32 devices in a mesh: tgt: 8 (over y, x, core), src: 4 (over z).
Axes of the slice: x: 2, y: 2, z: 4, core: 2. Of those that a mesh axis runs over, the one named last changes fastest.
Arguments:
- sources: bfloat16 [4, 1024, 32, 128], P('src', 'tgt'), may hold values from -6 to 6
- first_factors: bfloat16 [4, 1024, 2, 64, 128], P('src', 'tgt'), may hold values from -0.375 to 0.375
- second_factors: bfloat16 [1024, 2, 64, 128], P('tgt'), may hold values from -0.375 to 0.375
- pattern: int32 [1024], P('tgt'), may hold values from 0 to 127, as said below
Outputs:
- targets: float32 [1024, 32, 128], P(('tgt', 'src'))
The draws below stay inside these ranges and needn't reach their ends.
Inputs may be any that keep to these rules, and one draw needn't show every extreme that they name: Within each aligned group of 128 blocks, pattern is a permutation of 0 to 127.
All inputs are finite; a program needn't handle non-finite values.
Results may differ from the reference program's by a relative error of at most 0.0003.
Values may be sent and summed in bfloat16 or wider, within the bound.
No kernel may reach another device: no remote copies, remote signals or barrier semaphores. Data moves between devices by JAX's collectives and lax.ppermute only.
A program may use at most 64 MiB of HBM per device.

```python
import jax
import jax.numpy as jnp
from jax import lax

R = 64
RHS = 32
BD = 128
NB = 1024
NS = 4
N_TGT = 8


def draw_pattern(key, part):
    key = jax.random.fold_in(key, 11)
    group_keys = jax.random.split(key, NB // BD)
    orders = jax.vmap(lambda single: jax.random.permutation(single, BD))(group_keys)
    return orders.reshape(NB).astype(jnp.int32)


def level_of(stream_key, extent, pieces, least, top_value):
    def one(position, shards_of):
        steps = jax.random.uniform(jax.random.fold_in(jax.random.fold_in(stream_key, 6), position), (shards_of,), jnp.float32, least / len(pieces), top_value / len(pieces))
        return jnp.repeat(jnp.exp(steps), extent[position] // shards_of).reshape((-1,) + (1,) * (len(extent) - position - 1))

    factor_of = one(*pieces[0])
    for cut in pieces[1:]:
        factor_of = factor_of * one(*cut)
    return factor_of


def centred(rng, shape, deviation, limit, cuts=(), kind=jnp.bfloat16):
    factor_of = level_of(rng, shape, cuts, -0.22, 0.18) if cuts else 1.0
    result = jax.random.normal(rng, shape, jnp.float32) * deviation * factor_of
    return jnp.minimum(jnp.maximum(result, -limit), limit).astype(kind)


def setup_inputs(seed: int = 0) -> dict:
    keys = jax.random.split(jax.random.key(seed), 5)
    sources = centred(keys[0], (NS, NB, RHS, 2 * R), 1.0, 6.0, ((0, 4), (1, 8)))
    first_factors = centred(keys[1], (NS, NB, 2, R, 2 * R), (4 * R) ** -0.5, 0.375, ((0, 4), (1, 8)))
    second_factors = centred(keys[2], (NB, 2, R, 2 * R), (4 * R) ** -0.5, 0.375, ((0, 8),))
    pattern = draw_pattern(jax.random.fold_in(keys[4], 71), 0)
    return dict(sources=sources, first_factors=first_factors, second_factors=second_factors, pattern=pattern)


def apply_factor(values, factor, precise):
    blocks, rows, width = values.shape
    rank = width // 2
    split_values = values.reshape(blocks, rows, 2, rank)
    if precise:
        product = jnp.einsum("brck,bkj->brcj", split_values.astype(jnp.float32), factor.astype(jnp.float32), precision=lax.Precision.HIGHEST)
    else:
        product = jnp.einsum("brck,bkj->brcj", split_values.astype(jnp.float32), factor.astype(jnp.float32))
    real_part = product[:, :, 0, :rank] - product[:, :, 1, rank:]
    imag_part = product[:, :, 0, rank:] + product[:, :, 1, :rank]
    return jnp.concatenate([real_part, imag_part], axis=-1)


def reference(sources, first_factors, second_factors, pattern):
    blocks = jnp.arange(NB, dtype=jnp.int32)
    partner_one = ((blocks // BD) ^ (N_TGT // 2)) * BD + pattern.astype(jnp.int32)
    partner_two = blocks ^ (NB // 4)

    def add_quarter(total, index):
        values = sources[index]
        factors = first_factors[index]
        first = apply_factor(values, factors[:, 0], False) + apply_factor(values[partner_one], factors[:, 1], False)
        return total + first, None

    summed, unused = lax.scan(add_quarter, jnp.zeros((NB, RHS, 2 * R), jnp.float32), jnp.arange(NS, dtype=jnp.int32))
    return apply_factor(summed, second_factors[:, 0], True) + apply_factor(summed[partner_two], second_factors[:, 1], True)
```

```python
import functools

import jax
import jax.numpy as jnp
from jax import lax
from jax.experimental import pallas as pl
from jax.experimental.pallas import tpu as pltpu
from jax.sharding import PartitionSpec as P

CHUNKS = (8, 8, 8, 8)
VMEM = pl.BlockSpec(memory_space=pltpu.VMEM)
SMEM = pl.BlockSpec(memory_space=pltpu.SMEM)
PARAMS = pltpu.CompilerParams(vmem_limit_bytes=16 << 20)


def swapped(block, axis, mask):
    return lax.ppermute(block, axis, [(i, i ^ mask) for i in range(lax.axis_size(axis))])


def left_half(shape):
    return lax.broadcasted_iota(jnp.int32, shape, len(shape) - 1) < shape[-1] // 2


def stacked(own, partner):
    half = own.shape[-1] // 2
    left = left_half(own.shape)
    top = jnp.where(left, own, pltpu.roll(partner, half, 1))
    bottom = jnp.where(left, pltpu.roll(own, half, 1), partner)
    return jnp.concatenate([top, bottom], axis=0)


def folded(product):
    rows = product.shape[0] // 2
    turned = pltpu.roll(product[rows:], product.shape[1] // 2, 1)
    return product[:rows] + jnp.where(left_half(turned.shape), -turned, turned)


def encode(read, peak, out):
    count = out.shape[0] - 1
    exponent = jnp.floor(jnp.log2(jnp.maximum(peak, 1e-30))) + 1.0
    scale = jnp.exp2(15.0 - exponent)
    for i in range(count):
        code = jnp.clip(jnp.round(read(i) * scale), -32767.0, 32767.0)
        out[i] = code.astype(jnp.int32).astype(jnp.int16)
    out[count] = exponent.astype(jnp.int32).astype(jnp.int16)


def unit(coded):
    return jnp.exp2(coded[coded.shape[0] - 1].astype(jnp.float32) - 15.0)


def first_kernel(me_ref, pattern_ref, own_ref, partner_ref, factor_ref, *rest):
    *outs, total = rest
    me = me_ref[0]
    rows, width = own_ref.shape[1:]
    share = outs[0].shape[0]
    for turn in (*range(1, len(outs)), 0):
        base = (me ^ turn) * share
        out = outs[turn]
        peak = jnp.zeros((rows, width), jnp.float32)
        for i in range(share):
            own = own_ref[base + i].astype(jnp.float32)
            partner = partner_ref[pattern_ref[base + i]].astype(jnp.float32)
            values = stacked(own, partner).astype(jnp.bfloat16)
            factor = factor_ref[base + i].reshape(width, width)
            result = folded(jnp.dot(values, factor, preferred_element_type=jnp.float32))
            if turn == 0:
                out[i] = result
            else:
                total[turn - 1, i] = result
                peak = jnp.maximum(peak, jnp.abs(result))
        if turn:
            encode(lambda i: total[turn - 1, i], peak, out)


def first_level(me, pattern, own, partner, factors, parts):
    blocks, rows, width = own.shape
    share = blocks // parts
    coded = jax.ShapeDtypeStruct((share + 1, rows, width), jnp.int16)
    return pl.pallas_call(
        first_kernel,
        in_specs=[SMEM, SMEM, VMEM, VMEM, VMEM],
        out_specs=[VMEM] * parts,
        out_shape=[jax.ShapeDtypeStruct((share, rows, width), jnp.float32)] + [coded] * (parts - 1),
        scratch_shapes=[pltpu.VMEM((parts - 1, share, rows, width), jnp.float32)],
        compiler_params=PARAMS,
        name="first_level",
    )(me, pattern, own, partner, factors)


def sum_kernel(own_ref, *rest):
    *coded, total, out = rest
    units = [unit(c) for c in coded]
    peak = jnp.zeros(own_ref.shape[1:], jnp.float32)
    for i in range(own_ref.shape[0]):
        result = own_ref[i]
        for c, u in zip(coded, units):
            result = result + c[i].astype(jnp.float32) * u
        total[i] = result
        peak = jnp.maximum(peak, jnp.abs(result))
    encode(lambda i: total[i], peak, out)


def quarter_sum(own, coded):
    share, rows, width = own.shape
    return pl.pallas_call(
        sum_kernel,
        in_specs=[VMEM] * (1 + len(coded)),
        out_specs=[VMEM, VMEM],
        out_shape=[
            jax.ShapeDtypeStruct((share, rows, width), jnp.float32),
            jax.ShapeDtypeStruct((share + 1, rows, width), jnp.int16),
        ],
        compiler_params=PARAMS,
        name="quarter_sum",
    )(own, *coded)


def second_kernel(chunks, *refs):
    owns, partners, factor_ref, out = refs[:chunks], refs[chunks : 2 * chunks], refs[-2], refs[-1]
    width = out.shape[2]
    units = [unit(c) for c in partners]
    for i in range(out.shape[0]):
        own = jnp.concatenate([o[i] for o in owns], axis=0)
        partner = jnp.concatenate([c[i].astype(jnp.float32) * u for c, u in zip(partners, units)], axis=0)
        values = stacked(own, partner)
        high = values.astype(jnp.bfloat16)
        low = (values - high.astype(jnp.float32)).astype(jnp.bfloat16)
        factor = factor_ref[i].reshape(width, width)
        product = jnp.dot(jnp.concatenate([high, low], axis=0), factor, preferred_element_type=jnp.float32)
        out[i] = folded(product[: 2 * own.shape[0]] + product[2 * own.shape[0] :])


def second_level(owns, partners, factors):
    share, _, width = owns[0].shape
    rows = sum(o.shape[1] for o in owns)
    return pl.pallas_call(
        functools.partial(second_kernel, len(owns)),
        in_specs=[VMEM] * (2 * len(owns) + 1),
        out_specs=VMEM,
        out_shape=jax.ShapeDtypeStruct((share, rows, width), jnp.float32),
        compiler_params=PARAMS,
        name="second_level",
    )(*owns, *partners, factors)


def on_device(sources, first_factors, second_factors, pattern):
    half = lax.axis_size("tgt") // 2
    parts = lax.axis_size("src")
    sources, first_factors = sources[0], first_factors[0]
    share = sources.shape[0] // parts
    me = lax.axis_index("src").astype(jnp.int32)
    starts = [sum(CHUNKS[:c]) for c in range(len(CHUNKS))]
    values = [sources[:, start : start + rows] for start, rows in zip(starts, CHUNKS)]
    partners = [swapped(v, "tgt", half) for v in values]
    mine = lax.dynamic_slice_in_dim(second_factors, me * share, share, 0)
    owns, others = [], []
    for own, partner in zip(values, partners):
        kept, *sent = first_level(me.reshape(1), pattern, own, partner, first_factors, parts)
        arrived = [swapped(s, "src", turn + 1) for turn, s in enumerate(sent)]
        total, coded = quarter_sum(kept, arrived)
        owns.append(total)
        others.append(swapped(coded, "tgt", half // 2))
    return second_level(owns, others, mine)


def solution(mesh):
    return jax.shard_map(
        on_device,
        mesh=mesh,
        in_specs=(
            P("src", "tgt", None, None),
            P("src", "tgt", None, None, None),
            P("tgt", None, None, None),
            P("tgt"),
        ),
        out_specs=P(("tgt", "src"), None, None),
        check_vma=False,
    )
```

```python
import functools

import jax
import jax.numpy as jnp
from jax import lax
from jax.experimental import pallas as pl
from jax.experimental.pallas import tpu as pltpu
from jax.sharding import PartitionSpec as P

CHUNKS = (8, 8, 8, 8)
DIRECT = (0, 0, 0, 1)
VMEM = pl.BlockSpec(memory_space=pltpu.VMEM)
SMEM = pl.BlockSpec(memory_space=pltpu.SMEM)
ANY = pl.BlockSpec(memory_space=pl.ANY)
PARAMS = pltpu.CompilerParams(vmem_limit_bytes=16 << 20)


def swapped(block, axis, mask):
    return lax.ppermute(block, axis, [(i, i ^ mask) for i in range(lax.axis_size(axis))])


def left_half(shape):
    return lax.broadcasted_iota(jnp.int32, shape, len(shape) - 1) < shape[-1] // 2


def turned(values):
    return pltpu.roll(values, values.shape[-1] // 2, 1)


def halves(values):
    values = values.astype(jnp.float32)
    return jnp.concatenate([values, turned(values)], axis=0)[:, : values.shape[-1] // 2].astype(jnp.bfloat16)


def stacked(own, partner):
    left = left_half(own.shape)
    top = jnp.where(left, own, turned(partner))
    bottom = jnp.where(left, turned(own), partner)
    return jnp.concatenate([top, bottom], axis=0)


def folded(product):
    rows = product.shape[0] // 2
    other = turned(product[rows:])
    return product[:rows] + jnp.where(left_half(other.shape), -other, other)


def dot(a, b):
    return jnp.dot(a, b, preferred_element_type=jnp.float32)


def encode(read, peak, out, first, count, where=slice(None)):
    exponent = jnp.floor(jnp.log2(jnp.maximum(peak, 1e-30))) + 1.0
    scale = jnp.exp2(15.0 - exponent)
    for i in range(count):
        code = jnp.clip(jnp.round(read(i) * scale), -32767.0, 32767.0)
        out[first + i, where] = code.astype(jnp.int32).astype(jnp.int16)
    out[first + count, where] = exponent.astype(jnp.int32).astype(jnp.int16)


def decoder(coded, first, count):
    unit = jnp.exp2(coded[first + count].astype(jnp.float32) - 15.0)
    return lambda i: coded[first + i].astype(jnp.float32) * unit


def call(kernel, name, in_specs, outs, *args, after=(), **more):
    count = len(args)

    def body(*refs):
        kernel(*refs[:count], *refs[count + len(after) :])

    return pl.pallas_call(
        body,
        in_specs=in_specs + [ANY] * len(after),
        out_specs=[VMEM] * len(outs),
        out_shape=[jax.ShapeDtypeStruct(shape, kind) for shape, kind in outs],
        compiler_params=PARAMS,
        name=name,
        **more,
    )(*args, *after)


def rows_kernel(start, values_ref, *outs):
    for out in outs:
        rows = out.shape[1]
        out[...] = values_ref[:, pl.ds(start, rows)]
        start += rows


def rows_of(values, start, counts, after=()):
    blocks, _, width = values.shape
    outs = [((blocks, rows, width), values.dtype) for rows in counts]
    return call(functools.partial(rows_kernel, start), "rows_of", [VMEM], outs, values, after=after)


def own_kernel(chunks, *refs):
    values, factor_ref, outs, partner_factors = refs[:chunks], refs[chunks], refs[chunks + 1 : -1], refs[-1]
    for i in range(factor_ref.shape[0]):
        value = jnp.concatenate([v[i].astype(jnp.float32) for v in values], axis=0)
        result = folded(dot(halves(value), factor_ref[i, 0]))
        start = 0
        for out in outs:
            out[i] = result[start : start + out.shape[1]]
            start += out.shape[1]
        partner_factors[i] = factor_ref[i, 1]


def own_part(values, factors):
    blocks, _, rank, width = factors.shape
    outs = [(v.shape, jnp.float32) for v in values] + [((blocks, rank, width), factors.dtype)]
    *owns, partner_factors = call(
        functools.partial(own_kernel, len(values)), "own_part", [VMEM] * (len(values) + 1), outs, *values, factors
    )
    return owns, partner_factors


def partner_kernel(split, me_ref, pattern_ref, own_ref, partner_ref, factor_ref, kept, *rest):
    *outs, total = rest
    me = me_ref[0]
    share = kept.shape[1]
    rows, width = own_ref.shape[1:]

    def block(b):
        return own_ref[b] + folded(dot(halves(partner_ref[pattern_ref[b]]), factor_ref[b]))

    sent = [turn for turns in split for turn in turns]
    for out, turns in zip(outs, split):
        for place, turn in enumerate(turns):
            peak = jnp.zeros((rows, width), jnp.float32)
            held = total.at[sent.index(turn)]
            for i in range(share):
                result = block((me ^ turn) * share + i)
                held[i] = result
                peak = jnp.maximum(peak, jnp.abs(result))
            encode(lambda i: held[i], peak, out, place * (share + 1), share)
    stay = [turn for turn in range(len(sent) + kept.shape[0]) if turn not in sent]
    for place, turn in enumerate(stay):
        for i in range(share):
            kept[place, i] = block((me ^ turn) * share + i)


def partner_part(split, parts, me, pattern, own, partner, factors, after=()):
    blocks, rows, width = own.shape
    share = blocks // parts
    sent = sum(len(turns) for turns in split)
    outs = [((parts - sent, share, rows, width), jnp.float32)]
    outs += [((len(turns) * (share + 1), rows, width), jnp.int16) for turns in split]
    return call(
        functools.partial(partner_kernel, split),
        "partner_part",
        [SMEM, SMEM, VMEM, VMEM, VMEM],
        outs,
        me,
        pattern,
        own,
        partner,
        factors,
        after=after,
        scratch_shapes=[pltpu.VMEM((sent, share, rows, width), jnp.float32)],
    )


def halve_kernel(chunks, *refs):
    *ins, kept, out, total = refs
    half, share = kept.shape[:2]
    start = 0
    for kept_ref, coded_ref in zip(ins[:chunks], ins[chunks:]):
        rows, width = kept_ref.shape[2:]
        where = pl.ds(start, rows)
        for place in range(2 * half):
            read = decoder(coded_ref, place * (share + 1), share)
            peak = jnp.zeros((rows, width), jnp.float32)
            for i in range(share):
                result = kept_ref[place, i] + read(i)
                if place < half:
                    kept[place, i, where] = result
                else:
                    total[i, where] = result
                    peak = jnp.maximum(peak, jnp.abs(result))
            if place >= half:
                encode(lambda i: total[i, where], peak, out, (place - half) * (share + 1), share, where)
        start += rows


def halve(kept, coded, after=()):
    held, share, _, width = kept[0].shape
    rows = sum(k.shape[2] for k in kept)
    return call(
        functools.partial(halve_kernel, len(kept)),
        "halve",
        [VMEM] * (2 * len(kept)),
        [((held // 2, share, rows, width), jnp.float32), ((held // 2 * (share + 1), rows, width), jnp.int16)],
        *kept,
        *coded,
        after=after,
        scratch_shapes=[pltpu.VMEM((share, rows, width), jnp.float32)],
    )


def sum_kernel(counts, *refs):
    *ins, total, out = refs
    share = total.shape[0]
    start = 0
    for count in counts:
        kept, *coded = ins[: 1 + count]
        ins = ins[1 + count :]
        rows = kept.shape[2]
        reads = [decoder(c, 0, share) for c in coded]
        peak = jnp.zeros(kept.shape[2:], jnp.float32)
        where = pl.ds(start, rows)
        for i in range(share):
            result = kept[0, i]
            for read in reads:
                result = result + read(i)
            total[i, where] = result
            peak = jnp.maximum(peak, jnp.abs(result))
        encode(lambda i: total[i, where], peak, out, 0, share, where)
        start += rows


def quarter_sum(groups, after=()):
    _, share, _, width = groups[0][0].shape
    rows = sum(group[0].shape[2] for group in groups)
    args = [array for group in groups for array in group]
    return call(
        functools.partial(sum_kernel, [len(group) - 1 for group in groups]),
        "quarter_sum",
        [VMEM] * len(args),
        [((share, rows, width), jnp.float32), ((share + 1, rows, width), jnp.int16)],
        *args,
        after=after,
    )


def second_kernel(start, own_ref, coded_ref, factor_ref, *rest):
    out_hbm, out, semaphore = rest[-3:]
    share, rows, width = own_ref.shape
    read = decoder(coded_ref, 0, share)
    for i in range(share):
        values = stacked(own_ref[i], read(i))
        high = values.astype(jnp.bfloat16)
        low = (values - high.astype(jnp.float32)).astype(jnp.bfloat16)
        product = dot(jnp.concatenate([high, low], axis=0), factor_ref[i].reshape(width, width))
        out[i] = folded(product[: 2 * rows] + product[2 * rows :])
    copy = pltpu.make_async_copy(out, out_hbm.at[:, pl.ds(start, rows)], semaphore)
    copy.start()
    copy.wait()


def second_level(own, coded, factors, start, rows_in_all, result=None):
    share, rows, width = own.shape
    args = (own, coded, factors) if result is None else (own, coded, factors, result)
    return pl.pallas_call(
        functools.partial(second_kernel, start),
        in_specs=[VMEM] * 3 + [ANY] * (len(args) - 3),
        out_specs=ANY,
        out_shape=jax.ShapeDtypeStruct((share, rows_in_all, width), jnp.float32),
        scratch_shapes=[pltpu.VMEM((share, rows, width), jnp.float32), pltpu.SemaphoreType.DMA],
        input_output_aliases={} if result is None else {3: 0},
        compiler_params=PARAMS,
        name="second_level",
    )(*args)


def on_device(sources, first_factors, second_factors, pattern):
    half = lax.axis_size("tgt") // 2
    parts = lax.axis_size("src")
    sources, first_factors = sources[0], first_factors[0]
    blocks, rows_in_all, _ = sources.shape
    share = blocks // parts
    me = lax.axis_index("src").astype(jnp.int32)
    starts = [sum(CHUNKS[:c]) for c in range(len(CHUNKS))]
    values = rows_of(sources, 0, CHUNKS)
    partners = [swapped(v, "tgt", half) for v in values]
    owns, factors = own_part(values, first_factors)
    mine = lax.dynamic_slice_in_dim(second_factors, me * share, share, 0)
    waiting, marks = {}, {"mine": mine}
    order = [('first', (0,)), ('halve', (0,)), ('first', (1,), ('first', (0,))), ('halve', (1,)), ('first', (2,), ('first', (1,)), ('halve', (0,))), ('first', (3,), ('first', (2,)), ('halve', (1,))), ('halve', (2,), ('first', (3,)))]
    for step, chunks, *before in order:
        last = [marks[b] for b in before]
        if step == "first":
            (c,) = chunks
            turns = range(1, parts)
            split = [[turn] for turn in turns] if DIRECT[c] else [[turn for turn in turns if turn & 1]]
            kept, *coded = partner_part(split, parts, me.reshape(1), pattern, owns[c], partners[c], factors, last)
            masks = turns if DIRECT[c] else [1]
            arrived = [swapped(s, "src", mask) for s, mask in zip(coded, masks)]
            waiting[chunks] = (kept, *arrived)
        else:
            kept, coded = halve([waiting[(c,)][0] for c in chunks], [waiting[(c,)][1] for c in chunks], last)
            mask = 2
            arrived = swapped(coded, "src", mask)
            while 2 * mask < parts:
                mask *= 2
                kept, coded = halve([kept], [arrived])
                arrived = swapped(coded, "src", mask)
            waiting[chunks] = (kept, arrived)
        marks[step, chunks] = kept
    result, start = None, 0
    for part in [[(0,), (1,), (2,)], [(3,)]]:
        total, coded = quarter_sum([waiting[chunks] for chunks in part], ())
        other = swapped(coded, "tgt", half // 2)
        result = second_level(total, other, mine, start, rows_in_all, result)
        start += total.shape[1]
    return result


def solution(mesh):
    return jax.shard_map(
        on_device,
        mesh=mesh,
        in_specs=(
            P("src", "tgt", None, None),
            P("src", "tgt", None, None, None),
            P("tgt", None, None, None),
            P("tgt"),
        ),
        out_specs=P(("tgt", "src"), None, None),
        check_vma=False,
    )
```

```python
import functools

import jax
import jax.numpy as jnp
from jax import lax
from jax.experimental import pallas as pl
from jax.experimental.pallas import tpu as pltpu
from jax.sharding import PartitionSpec as P

CHUNKS = (8, 8, 8, 8)
DIRECT = (0, 0, 0, 1)
GROUP = 8
PACK = 4
VMEM = pl.BlockSpec(memory_space=pltpu.VMEM)
SMEM = pl.BlockSpec(memory_space=pltpu.SMEM)
ANY = pl.BlockSpec(memory_space=pl.ANY)
PARAMS = pltpu.CompilerParams(vmem_limit_bytes=16 << 20)


def swapped(block, axis, mask):
    return lax.ppermute(block, axis, [(i, i ^ mask) for i in range(lax.axis_size(axis))])


def left_half(shape):
    return lax.broadcasted_iota(jnp.int32, shape, len(shape) - 1) < shape[-1] // 2


def turned(values):
    return pltpu.roll(values, values.shape[-1] // 2, 1)


def halves(values):
    values = values.astype(jnp.float32)
    return jnp.concatenate([values, turned(values)], axis=0)[:, : values.shape[-1] // 2].astype(jnp.bfloat16)


def stacked(own, partner):
    left = left_half(own.shape)
    top = jnp.where(left, own, turned(partner))
    bottom = jnp.where(left, turned(own), partner)
    return jnp.concatenate([top, bottom], axis=0)


def folded(product):
    rows = product.shape[0] // 2
    other = turned(product[rows:])
    return product[:rows] + jnp.where(left_half(other.shape), -other, other)


def dot(a, b):
    return jnp.dot(a, b, preferred_element_type=jnp.float32)


def encode(read, peak, out, first, count, where=slice(None)):
    exponent = jnp.floor(jnp.log2(jnp.maximum(peak, 1e-30))) + 1.0
    scale = jnp.exp2(15.0 - exponent)
    for i in range(count):
        code = jnp.clip(jnp.round(read(i) * scale), -32767.0, 32767.0)
        out[first + i, where] = code.astype(jnp.int32).astype(jnp.int16)
    out[first + count, where] = exponent.astype(jnp.int32).astype(jnp.int16)


def decoder(coded, first, count):
    unit = jnp.exp2(coded[first + count].astype(jnp.float32) - 15.0)
    return lambda i: coded[first + i].astype(jnp.float32) * unit


def call(kernel, name, in_specs, outs, *args, after=(), **more):
    count = len(args)

    def body(*refs):
        kernel(*refs[:count], *refs[count + len(after) :])

    return pl.pallas_call(
        body,
        in_specs=in_specs + [ANY] * len(after),
        out_specs=[VMEM] * len(outs),
        out_shape=[jax.ShapeDtypeStruct(shape, kind) for shape, kind in outs],
        compiler_params=PARAMS,
        name=name,
        **more,
    )(*args, *after)


def rows_kernel(start, values_ref, *outs):
    for out in outs:
        rows = out.shape[1]
        out[...] = values_ref[:, pl.ds(start, rows)]
        start += rows


def rows_of(values, start, counts, after=()):
    blocks, _, width = values.shape
    outs = [((blocks, rows, width), values.dtype) for rows in counts]
    return call(functools.partial(rows_kernel, start), "rows_of", [VMEM], outs, values, after=after)


def own_kernel(chunks, *refs):
    values, factor_ref, outs, partner_factors = refs[:chunks], refs[chunks], refs[chunks + 1 : -1], refs[-1]
    for i in range(factor_ref.shape[0]):
        value = jnp.concatenate([v[i].astype(jnp.float32) for v in values], axis=0)
        result = folded(dot(halves(value), factor_ref[i, 0]))
        start = 0
        for out in outs:
            out[i] = result[start : start + out.shape[1]]
            start += out.shape[1]
        partner_factors[i] = factor_ref[i, 1]


def own_part(values, factors):
    blocks, _, rank, width = factors.shape
    outs = [(v.shape, jnp.float32) for v in values] + [((blocks, rank, width), factors.dtype)]
    *owns, partner_factors = call(
        functools.partial(own_kernel, len(values)), "own_part", [VMEM] * (len(values) + 1), outs, *values, factors
    )
    return owns, partner_factors


def partner_kernel(split, pattern_ref, own_ref, partner_ref, factor_ref, kept, *rest):
    *outs, total = rest
    me = lax.axis_index("src")
    share = kept.shape[1]
    rows, width = own_ref.shape[1:]

    left = left_half((rows, width))
    zero = jnp.zeros((2 * rows, width), jnp.bfloat16)

    def blocks(base):
        values = []
        for j in range(PACK):
            value = partner_ref[pattern_ref[base + j]].astype(jnp.float32)
            pair, side = ((value, turned(value)), left) if j % 2 == 0 else ((turned(value), value), ~left)
            column = jnp.concatenate([jnp.where(side, v, 0.0) for v in pair], axis=0).astype(jnp.bfloat16)
            values.append(jnp.concatenate([column if k == j // 2 else zero for k in range(PACK // 2)], axis=1))
        factor = factor_ref[pl.ds(base, PACK)].reshape(PACK * (width // 2), width)
        product = dot(jnp.concatenate(values, axis=0), factor)
        return [own_ref[base + j] + folded(product[2 * rows * j : 2 * rows * (j + 1)]) for j in range(PACK)]

    sent = [turn for turns in split for turn in turns]
    for out, turns in zip(outs, split):
        for place, turn in enumerate(turns):
            peak = jnp.zeros((rows, width), jnp.float32)
            held = total.at[sent.index(turn)]
            for i in range(0, share, PACK):
                for j, result in enumerate(blocks((me ^ turn) * share + i)):
                    held[i + j] = result
                    peak = jnp.maximum(peak, jnp.abs(result))
            encode(lambda i: held[i], peak, out, place * (share + 1), share)
    stay = [turn for turn in range(len(sent) + kept.shape[0]) if turn not in sent]
    for place, turn in enumerate(stay):
        for i in range(0, share, PACK):
            for j, result in enumerate(blocks((me ^ turn) * share + i)):
                kept[place, i + j] = result


def partner_part(split, parts, pattern, own, partner, factors, after=()):
    blocks, rows, width = own.shape
    share = blocks // parts
    sent = sum(len(turns) for turns in split)
    outs = [((parts - sent, share, rows, width), jnp.float32)]
    outs += [((len(turns) * (share + 1), rows, width), jnp.int16) for turns in split]
    return call(
        functools.partial(partner_kernel, split),
        "partner_part",
        [SMEM, VMEM, VMEM, VMEM],
        outs,
        pattern,
        own,
        partner,
        factors,
        after=after,
        scratch_shapes=[pltpu.VMEM((sent, share, rows, width), jnp.float32)],
    )


def halve_kernel(chunks, *refs):
    *ins, kept, out, total = refs
    half, share = kept.shape[:2]
    start = 0
    for kept_ref, coded_ref in zip(ins[:chunks], ins[chunks:]):
        rows, width = kept_ref.shape[2:]
        where = pl.ds(start, rows)
        for place in range(2 * half):
            read = decoder(coded_ref, place * (share + 1), share)
            peak = jnp.zeros((rows, width), jnp.float32)
            for i in range(share):
                result = kept_ref[place, i] + read(i)
                if place < half:
                    kept[place, i, where] = result
                else:
                    total[i, where] = result
                    peak = jnp.maximum(peak, jnp.abs(result))
            if place >= half:
                encode(lambda i: total[i, where], peak, out, (place - half) * (share + 1), share, where)
        start += rows


def halve(kept, coded, after=()):
    held, share, _, width = kept[0].shape
    rows = sum(k.shape[2] for k in kept)
    return call(
        functools.partial(halve_kernel, len(kept)),
        "halve",
        [VMEM] * (2 * len(kept)),
        [((held // 2, share, rows, width), jnp.float32), ((held // 2 * (share + 1), rows, width), jnp.int16)],
        *kept,
        *coded,
        after=after,
        scratch_shapes=[pltpu.VMEM((share, rows, width), jnp.float32)],
    )


def sum_kernel(counts, *refs):
    *ins, total, out = refs
    share = total.shape[0]
    start = 0
    for count in counts:
        kept, *coded = ins[: 1 + count]
        ins = ins[1 + count :]
        rows = kept.shape[2]
        reads = [decoder(c, 0, share) for c in coded]
        peak = jnp.zeros(kept.shape[2:], jnp.float32)
        where = pl.ds(start, rows)
        for i in range(share):
            result = kept[0, i]
            for read in reads:
                result = result + read(i)
            total[i, where] = result
            peak = jnp.maximum(peak, jnp.abs(result))
        encode(lambda i: total[i, where], peak, out, 0, share, where)
        start += rows


def quarter_sum(groups, after=()):
    _, share, _, width = groups[0][0].shape
    rows = sum(group[0].shape[2] for group in groups)
    args = [array for group in groups for array in group]
    return call(
        functools.partial(sum_kernel, [len(group) - 1 for group in groups]),
        "quarter_sum",
        [VMEM] * len(args),
        [((share, rows, width), jnp.float32), ((share + 1, rows, width), jnp.int16)],
        *args,
        after=after,
    )


def second_kernel(start, own_ref, coded_ref, factor_ref, *rest):
    out_hbm, out, semaphore = rest[-3:]
    share, rows, width = own_ref.shape
    read = decoder(coded_ref, 0, share)
    copies = []
    for i in range(share):
        values = stacked(own_ref[i], read(i))
        high = values.astype(jnp.bfloat16)
        low = (values - high.astype(jnp.float32)).astype(jnp.bfloat16)
        product = dot(jnp.concatenate([high, low], axis=0), factor_ref[i].reshape(width, width))
        out[i] = folded(product[: 2 * rows] + product[2 * rows :])
        if (i + 1) % GROUP == 0:
            some = pl.ds(i + 1 - GROUP, GROUP)
            copy = pltpu.make_async_copy(
                out.at[some], out_hbm.at[some, pl.ds(start, rows)], semaphore.at[i // GROUP]
            )
            copy.start()
            copies.append(copy)
    for copy in copies:
        copy.wait()


def second_level(own, coded, factors, start, rows_in_all, result=None):
    share, rows, width = own.shape
    args = (own, coded, factors) if result is None else (own, coded, factors, result)
    return pl.pallas_call(
        functools.partial(second_kernel, start),
        in_specs=[VMEM] * 3 + [ANY] * (len(args) - 3),
        out_specs=ANY,
        out_shape=jax.ShapeDtypeStruct((share, rows_in_all, width), jnp.float32),
        scratch_shapes=[pltpu.VMEM((share, rows, width), jnp.float32), pltpu.SemaphoreType.DMA((share // GROUP,))],
        input_output_aliases={} if result is None else {3: 0},
        compiler_params=PARAMS,
        name="second_level",
    )(*args)


def on_device(sources, first_factors, second_factors, pattern):
    half = lax.axis_size("tgt") // 2
    parts = lax.axis_size("src")
    sources, first_factors = sources[0], first_factors[0]
    blocks, rows_in_all, _ = sources.shape
    share = blocks // parts
    me = lax.axis_index("src").astype(jnp.int32)
    starts = [sum(CHUNKS[:c]) for c in range(len(CHUNKS))]
    values = [sources[:, : CHUNKS[0]]]
    values += rows_of(sources, CHUNKS[0], CHUNKS[1:], values)
    partners = [swapped(v, "tgt", half) for v in values]
    owns, factors = own_part(values, first_factors)
    mine = lax.dynamic_slice_in_dim(second_factors, me * share, share, 0)
    waiting, marks = {}, {"mine": mine}
    order = [('first', (0,)), ('first', (1,), ('first', (0,))), ('first', (2,), ('first', (1,))), ('halve', (0, 1), ('first', (2,))), ('first', (3,), ('first', (2,)), ('halve', (0, 1))), ('halve', (2,), ('first', (3,)))]
    for step, chunks, *before in order:
        last = [marks[b] for b in before]
        if step == "first":
            (c,) = chunks
            turns = range(1, parts)
            split = [[turn] for turn in turns] if DIRECT[c] else [[turn for turn in turns if turn & 1]]
            kept, *coded = partner_part(split, parts, pattern, owns[c], partners[c], factors, last)
            masks = turns if DIRECT[c] else [1]
            arrived = [swapped(s, "src", mask) for s, mask in zip(coded, masks)]
            waiting[chunks] = (kept, *arrived)
        else:
            kept, coded = halve([waiting[(c,)][0] for c in chunks], [waiting[(c,)][1] for c in chunks], last)
            mask = 2
            arrived = swapped(coded, "src", mask)
            while 2 * mask < parts:
                mask *= 2
                kept, coded = halve([kept], [arrived])
                arrived = swapped(coded, "src", mask)
            waiting[chunks] = (kept, arrived)
        marks[step, chunks] = kept
        marks["arrived", chunks] = waiting[chunks][1]
    result, start = None, 0
    for part in [[(0, 1), (2,)], [(3,)]]:
        total, coded = quarter_sum([waiting[chunks] for chunks in part], ())
        other = swapped(coded, "tgt", half // 2)
        result = second_level(total, other, mine, start, rows_in_all, result)
        start += total.shape[1]
    return result


def solution(mesh):
    return jax.shard_map(
        on_device,
        mesh=mesh,
        in_specs=(
            P("src", "tgt", None, None),
            P("src", "tgt", None, None, None),
            P("tgt", None, None, None),
            P("tgt"),
        ),
        out_specs=P(("tgt", "src"), None, None),
        check_vma=False,
    )
```

```python
import functools

import jax
import jax.numpy as jnp
from jax import lax
from jax.experimental import pallas as pl
from jax.experimental.pallas import tpu as pltpu
from jax.sharding import PartitionSpec as P

CHUNKS = (8, 8, 8, 8)
DIRECT = (0, 0, 0, 1)
GROUP = 8
PACK = 4
VMEM = pl.BlockSpec(memory_space=pltpu.VMEM)
SMEM = pl.BlockSpec(memory_space=pltpu.SMEM)
ANY = pl.BlockSpec(memory_space=pl.ANY)
PARAMS = pltpu.CompilerParams(vmem_limit_bytes=16 << 20)


def swapped(block, axis, mask):
    return lax.ppermute(block, axis, [(i, i ^ mask) for i in range(lax.axis_size(axis))])


def left_half(shape):
    return lax.broadcasted_iota(jnp.int32, shape, len(shape) - 1) < shape[-1] // 2


def turned(values):
    return pltpu.roll(values, values.shape[-1] // 2, 1)


def halves(values):
    values = values.astype(jnp.float32)
    return jnp.concatenate([values, turned(values)], axis=0)[:, : values.shape[-1] // 2].astype(jnp.bfloat16)


def stacked(own, partner):
    left = left_half(own.shape)
    top = jnp.where(left, own, turned(partner))
    bottom = jnp.where(left, turned(own), partner)
    return jnp.concatenate([top, bottom], axis=0)


def folded(product):
    rows = product.shape[0] // 2
    other = turned(product[rows:])
    return product[:rows] + jnp.where(left_half(other.shape), -other, other)


def dot(a, b):
    return jnp.dot(a, b, preferred_element_type=jnp.float32)


def encode(read, peak, out, first, count, where=slice(None)):
    exponent = jnp.floor(jnp.log2(jnp.maximum(peak, 1e-30))) + 1.0
    scale = jnp.exp2(15.0 - exponent)
    for i in range(count):
        code = jnp.clip(jnp.round(read(i) * scale), -32767.0, 32767.0)
        out[first + i, where] = code.astype(jnp.int32).astype(jnp.int16)
    out[first + count, where] = exponent.astype(jnp.int32).astype(jnp.int16)


def decoder(coded, first, count):
    unit = jnp.exp2(coded[first + count].astype(jnp.float32) - 15.0)
    return lambda i: coded[first + i].astype(jnp.float32) * unit


def call(kernel, name, in_specs, outs, *args, after=(), **more):
    count = len(args)

    def body(*refs):
        kernel(*refs[:count], *refs[count + len(after) :])

    return pl.pallas_call(
        body,
        in_specs=in_specs + [ANY] * len(after),
        out_specs=[VMEM] * len(outs),
        out_shape=[jax.ShapeDtypeStruct(shape, kind) for shape, kind in outs],
        compiler_params=PARAMS,
        name=name,
        **more,
    )(*args, *after)


def rows_kernel(start, values_ref, *outs):
    for out in outs:
        rows = out.shape[1]
        out[...] = values_ref[:, pl.ds(start, rows)]
        start += rows


def rows_of(values, start, counts, after=()):
    blocks, _, width = values.shape
    outs = [((blocks, rows, width), values.dtype) for rows in counts]
    return call(functools.partial(rows_kernel, start), "rows_of", [VMEM], outs, values, after=after)


def own_kernel(chunks, *refs):
    values, factor_ref, outs, partner_factors = refs[:chunks], refs[chunks], refs[chunks + 1 : -1], refs[-1]
    for i in range(factor_ref.shape[0]):
        value = jnp.concatenate([v[i].astype(jnp.float32) for v in values], axis=0)
        result = folded(dot(halves(value), factor_ref[i, 0]))
        start = 0
        for out in outs:
            out[i] = result[start : start + out.shape[1]]
            start += out.shape[1]
        partner_factors[i] = factor_ref[i, 1]


def own_part(values, factors):
    blocks, _, rank, width = factors.shape
    outs = [(v.shape, jnp.float32) for v in values] + [((blocks, rank, width), factors.dtype)]
    *owns, partner_factors = call(
        functools.partial(own_kernel, len(values)), "own_part", [VMEM] * (len(values) + 1), outs, *values, factors
    )
    return owns, partner_factors


def partner_kernel(split, pattern_ref, own_ref, partner_ref, factor_ref, kept, *rest):
    *outs, total = rest
    me = lax.axis_index("src")
    share = kept.shape[1]
    rows, width = own_ref.shape[1:]

    left = left_half((rows, width))
    zero = jnp.zeros((2 * rows, width), jnp.bfloat16)

    def blocks(base):
        values = []
        for j in range(PACK):
            value = partner_ref[pattern_ref[base + j]].astype(jnp.float32)
            pair, side = ((value, turned(value)), left) if j % 2 == 0 else ((turned(value), value), ~left)
            column = jnp.concatenate([jnp.where(side, v, 0.0) for v in pair], axis=0).astype(jnp.bfloat16)
            values.append(jnp.concatenate([column if k == j // 2 else zero for k in range(PACK // 2)], axis=1))
        factor = factor_ref[pl.ds(base, PACK)].reshape(PACK * (width // 2), width)
        product = dot(jnp.concatenate(values, axis=0), factor)
        return [own_ref[base + j] + folded(product[2 * rows * j : 2 * rows * (j + 1)]) for j in range(PACK)]

    sent = [turn for turns in split for turn in turns]
    for out, turns in zip(outs, split):
        for place, turn in enumerate(turns):
            peak = jnp.zeros((rows, width), jnp.float32)
            held = total.at[sent.index(turn)]
            for i in range(0, share, PACK):
                for j, result in enumerate(blocks((me ^ turn) * share + i)):
                    held[i + j] = result
                    peak = jnp.maximum(peak, jnp.abs(result))
            encode(lambda i: held[i], peak, out, place * (share + 1), share)
    stay = [turn for turn in range(len(sent) + kept.shape[0]) if turn not in sent]
    for place, turn in enumerate(stay):
        for i in range(0, share, PACK):
            for j, result in enumerate(blocks((me ^ turn) * share + i)):
                kept[place, i + j] = result


def partner_part(split, parts, pattern, own, partner, factors, after=()):
    blocks, rows, width = own.shape
    share = blocks // parts
    sent = sum(len(turns) for turns in split)
    outs = [((parts - sent, share, rows, width), jnp.float32)]
    outs += [((len(turns) * (share + 1), rows, width), jnp.int16) for turns in split]
    return call(
        functools.partial(partner_kernel, split),
        "partner_part",
        [SMEM, VMEM, VMEM, VMEM],
        outs,
        pattern,
        own,
        partner,
        factors,
        after=after,
        scratch_shapes=[pltpu.VMEM((sent, share, rows, width), jnp.float32)],
    )


def halve_kernel(chunks, *refs):
    *ins, kept, out, total = refs
    half, share = kept.shape[:2]
    start = 0
    for kept_ref, coded_ref in zip(ins[:chunks], ins[chunks:]):
        rows, width = kept_ref.shape[2:]
        where = pl.ds(start, rows)
        for place in range(2 * half):
            read = decoder(coded_ref, place * (share + 1), share)
            peak = jnp.zeros((rows, width), jnp.float32)
            for i in range(share):
                result = kept_ref[place, i] + read(i)
                if place < half:
                    kept[place, i, where] = result
                else:
                    total[i, where] = result
                    peak = jnp.maximum(peak, jnp.abs(result))
            if place >= half:
                encode(lambda i: total[i, where], peak, out, (place - half) * (share + 1), share, where)
        start += rows


def halve(kept, coded, after=()):
    held, share, _, width = kept[0].shape
    rows = sum(k.shape[2] for k in kept)
    return call(
        functools.partial(halve_kernel, len(kept)),
        "halve",
        [VMEM] * (2 * len(kept)),
        [((held // 2, share, rows, width), jnp.float32), ((held // 2 * (share + 1), rows, width), jnp.int16)],
        *kept,
        *coded,
        after=after,
        scratch_shapes=[pltpu.VMEM((share, rows, width), jnp.float32)],
    )


def sum_kernel(counts, *refs):
    *ins, total, out = refs
    share = total.shape[0]
    start = 0
    for count in counts:
        kept, *coded = ins[: 1 + count]
        ins = ins[1 + count :]
        rows = kept.shape[2]
        reads = [decoder(c, 0, share) for c in coded]
        peak = jnp.zeros(kept.shape[2:], jnp.float32)
        where = pl.ds(start, rows)
        for i in range(share):
            result = kept[0, i]
            for read in reads:
                result = result + read(i)
            total[i, where] = result
            peak = jnp.maximum(peak, jnp.abs(result))
        encode(lambda i: total[i, where], peak, out, 0, share, where)
        start += rows


def quarter_sum(groups, after=()):
    _, share, _, width = groups[0][0].shape
    rows = sum(group[0].shape[2] for group in groups)
    args = [array for group in groups for array in group]
    return call(
        functools.partial(sum_kernel, [len(group) - 1 for group in groups]),
        "quarter_sum",
        [VMEM] * len(args),
        [((share, rows, width), jnp.float32), ((share + 1, rows, width), jnp.int16)],
        *args,
        after=after,
    )


def second_kernel(start, own_ref, coded_ref, factor_ref, *rest):
    out_hbm, out, semaphore = rest[-3:]
    share, rows, width = own_ref.shape
    read = decoder(coded_ref, 0, share)
    copies = []
    for i in range(share):
        values = stacked(own_ref[i], read(i))
        high = values.astype(jnp.bfloat16)
        low = (values - high.astype(jnp.float32)).astype(jnp.bfloat16)
        product = dot(jnp.concatenate([high, low], axis=0), factor_ref[i].reshape(width, width))
        out[i] = folded(product[: 2 * rows] + product[2 * rows :])
        if (i + 1) % GROUP == 0:
            some = pl.ds(i + 1 - GROUP, GROUP)
            copy = pltpu.make_async_copy(
                out.at[some], out_hbm.at[some, pl.ds(start, rows)], semaphore.at[i // GROUP]
            )
            copy.start()
            copies.append(copy)
    for copy in copies:
        copy.wait()


def second_level(own, coded, factors, start, rows_in_all, result=None):
    share, rows, width = own.shape
    args = (own, coded, factors) if result is None else (own, coded, factors, result)
    return pl.pallas_call(
        functools.partial(second_kernel, start),
        in_specs=[VMEM] * 3 + [ANY] * (len(args) - 3),
        out_specs=ANY,
        out_shape=jax.ShapeDtypeStruct((share, rows_in_all, width), jnp.float32),
        scratch_shapes=[pltpu.VMEM((share, rows, width), jnp.float32), pltpu.SemaphoreType.DMA((share // GROUP,))],
        input_output_aliases={} if result is None else {3: 0},
        compiler_params=PARAMS,
        name="second_level",
    )(*args)


def on_device(sources, first_factors, second_factors, pattern):
    half = lax.axis_size("tgt") // 2
    parts = lax.axis_size("src")
    sources, first_factors = sources[0], first_factors[0]
    blocks, rows_in_all, _ = sources.shape
    share = blocks // parts
    me = lax.axis_index("src").astype(jnp.int32)
    starts = [sum(CHUNKS[:c]) for c in range(len(CHUNKS))]
    values = [sources[:, : CHUNKS[0]]]
    values += rows_of(sources, CHUNKS[0], CHUNKS[1:], values)
    partners = [swapped(v, "tgt", half) for v in values]
    owns, factors = own_part(values, first_factors)
    mine = lax.dynamic_slice_in_dim(second_factors, me * share, share, 0)
    waiting, marks = {}, {"mine": mine}
    order = [('first', (0,)), ('first', (1,), ('first', (0,))), ('first', (2,), ('first', (1,))), ('halve', (0, 1), ('first', (2,))), ('first', (3,), ('first', (2,))), ('halve', (2,), ('first', (3,)))]
    for step, chunks, *before in order:
        last = [marks[b] for b in before]
        if step == "first":
            (c,) = chunks
            turns = range(1, parts)
            split = [[turn] for turn in turns] if DIRECT[c] else [[turn for turn in turns if turn & 1]]
            kept, *coded = partner_part(split, parts, pattern, owns[c], partners[c], factors, last)
            masks = turns if DIRECT[c] else [1]
            arrived = [swapped(s, "src", mask) for s, mask in zip(coded, masks)]
            waiting[chunks] = (kept, *arrived)
        else:
            kept, coded = halve([waiting[(c,)][0] for c in chunks], [waiting[(c,)][1] for c in chunks], last)
            mask = 2
            arrived = swapped(coded, "src", mask)
            while 2 * mask < parts:
                mask *= 2
                kept, coded = halve([kept], [arrived])
                arrived = swapped(coded, "src", mask)
            waiting[chunks] = (kept, arrived)
        marks[step, chunks] = kept
        marks["arrived", chunks] = waiting[chunks][1]
    result, start = None, 0
    for part in [[(0, 1), (2,)], [(3,)]]:
        total, coded = quarter_sum([waiting[chunks] for chunks in part], ())
        other = swapped(coded, "tgt", half // 2)
        result = second_level(total, other, mine, start, rows_in_all, result)
        start += total.shape[1]
    return result


def solution(mesh):
    return jax.shard_map(
        on_device,
        mesh=mesh,
        in_specs=(
            P("src", "tgt", None, None),
            P("src", "tgt", None, None, None),
            P("tgt", None, None, None),
            P("tgt"),
        ),
        out_specs=P(("tgt", "src"), None, None),
        check_vma=False,
    )
```

```python
import functools

import jax
import jax.numpy as jnp
from jax import lax
from jax.experimental import pallas as pl
from jax.experimental.pallas import tpu as pltpu
from jax.sharding import PartitionSpec as P

CHUNKS = (8, 8, 8, 8)
DIRECT = (0, 0, 0, 1)
GROUP = 8
PACK = 4
VMEM = pl.BlockSpec(memory_space=pltpu.VMEM)
SMEM = pl.BlockSpec(memory_space=pltpu.SMEM)
ANY = pl.BlockSpec(memory_space=pl.ANY)
PARAMS = pltpu.CompilerParams(vmem_limit_bytes=16 << 20)


def swapped(block, axis, mask):
    return lax.ppermute(block, axis, [(i, i ^ mask) for i in range(lax.axis_size(axis))])


def left_half(shape):
    return lax.broadcasted_iota(jnp.int32, shape, len(shape) - 1) < shape[-1] // 2


def turned(values):
    return pltpu.roll(values, values.shape[-1] // 2, 1)


def halves(values):
    values = values.astype(jnp.float32)
    return jnp.concatenate([values, turned(values)], axis=0)[:, : values.shape[-1] // 2].astype(jnp.bfloat16)


def stacked(own, partner):
    left = left_half(own.shape)
    top = jnp.where(left, own, turned(partner))
    bottom = jnp.where(left, turned(own), partner)
    return jnp.concatenate([top, bottom], axis=0)


def folded(product):
    rows = product.shape[0] // 2
    other = turned(product[rows:])
    return product[:rows] + jnp.where(left_half(other.shape), -other, other)


def dot(a, b):
    return jnp.dot(a, b, preferred_element_type=jnp.float32)


def encode(read, peak, out, first, count, where=slice(None)):
    exponent = jnp.floor(jnp.log2(jnp.maximum(peak, 1e-30))) + 1.0
    scale = jnp.exp2(15.0 - exponent)
    for i in range(count):
        code = jnp.clip(jnp.round(read(i) * scale), -32767.0, 32767.0)
        out[first + i, where] = code.astype(jnp.int32).astype(jnp.int16)
    out[first + count, where] = exponent.astype(jnp.int32).astype(jnp.int16)


def decoder(coded, first, count):
    unit = jnp.exp2(coded[first + count].astype(jnp.float32) - 15.0)
    return lambda i: coded[first + i].astype(jnp.float32) * unit


def call(kernel, name, in_specs, outs, *args, after=(), **more):
    count = len(args)

    def body(*refs):
        kernel(*refs[:count], *refs[count + len(after) :])

    return pl.pallas_call(
        body,
        in_specs=in_specs + [ANY] * len(after),
        out_specs=[VMEM] * len(outs),
        out_shape=[jax.ShapeDtypeStruct(shape, kind) for shape, kind in outs],
        compiler_params=PARAMS,
        name=name,
        **more,
    )(*args, *after)


def rows_kernel(start, values_ref, *outs):
    for out in outs:
        rows = out.shape[1]
        out[...] = values_ref[:, pl.ds(start, rows)]
        start += rows


def rows_of(values, start, counts, after=()):
    blocks, _, width = values.shape
    outs = [((blocks, rows, width), values.dtype) for rows in counts]
    return call(functools.partial(rows_kernel, start), "rows_of", [VMEM], outs, values, after=after)


def own_kernel(chunks, *refs):
    values, factor_ref, outs, partner_factors = refs[:chunks], refs[chunks], refs[chunks + 1 : -1], refs[-1]
    for i in range(factor_ref.shape[0]):
        value = jnp.concatenate([v[i].astype(jnp.float32) for v in values], axis=0)
        result = folded(dot(halves(value), factor_ref[i, 0]))
        start = 0
        for out in outs:
            out[i] = result[start : start + out.shape[1]]
            start += out.shape[1]
        partner_factors[i] = factor_ref[i, 1]


def own_part(values, factors):
    blocks, _, rank, width = factors.shape
    outs = [(v.shape, jnp.float32) for v in values] + [((blocks, rank, width), factors.dtype)]
    *owns, partner_factors = call(
        functools.partial(own_kernel, len(values)), "own_part", [VMEM] * (len(values) + 1), outs, *values, factors
    )
    return owns, partner_factors


def partner_kernel(split, pattern_ref, own_ref, partner_ref, factor_ref, kept, *rest):
    *outs, total = rest
    me = lax.axis_index("src")
    share = kept.shape[1]
    rows, width = own_ref.shape[1:]

    left = left_half((rows, width))
    zero = jnp.zeros((2 * rows, width), jnp.bfloat16)

    def blocks(base):
        values = []
        for j in range(PACK):
            value = partner_ref[pattern_ref[base + j]].astype(jnp.float32)
            pair, side = ((value, turned(value)), left) if j % 2 == 0 else ((turned(value), value), ~left)
            column = jnp.concatenate([jnp.where(side, v, 0.0) for v in pair], axis=0).astype(jnp.bfloat16)
            values.append(jnp.concatenate([column if k == j // 2 else zero for k in range(PACK // 2)], axis=1))
        factor = factor_ref[pl.ds(base, PACK)].reshape(PACK * (width // 2), width)
        product = dot(jnp.concatenate(values, axis=0), factor)
        return [own_ref[base + j] + folded(product[2 * rows * j : 2 * rows * (j + 1)]) for j in range(PACK)]

    sent = [turn for turns in split for turn in turns]
    for out, turns in zip(outs, split):
        for place, turn in enumerate(turns):
            peak = jnp.zeros((rows, width), jnp.float32)
            held = total.at[sent.index(turn)]
            for i in range(0, share, PACK):
                for j, result in enumerate(blocks((me ^ turn) * share + i)):
                    held[i + j] = result
                    peak = jnp.maximum(peak, jnp.abs(result))
            encode(lambda i: held[i], peak, out, place * (share + 1), share)
    stay = [turn for turn in range(len(sent) + kept.shape[0]) if turn not in sent]
    for place, turn in enumerate(stay):
        for i in range(0, share, PACK):
            for j, result in enumerate(blocks((me ^ turn) * share + i)):
                kept[place, i + j] = result


def partner_part(split, parts, pattern, own, partner, factors, after=()):
    blocks, rows, width = own.shape
    share = blocks // parts
    sent = sum(len(turns) for turns in split)
    outs = [((parts - sent, share, rows, width), jnp.float32)]
    outs += [((len(turns) * (share + 1), rows, width), jnp.int16) for turns in split]
    return call(
        functools.partial(partner_kernel, split),
        "partner_part",
        [SMEM, VMEM, VMEM, VMEM],
        outs,
        pattern,
        own,
        partner,
        factors,
        after=after,
        scratch_shapes=[pltpu.VMEM((sent, share, rows, width), jnp.float32)],
    )


def halve_kernel(chunks, *refs):
    *ins, kept, out, total = refs
    half, share = kept.shape[:2]
    start = 0
    for kept_ref, coded_ref in zip(ins[:chunks], ins[chunks:]):
        rows, width = kept_ref.shape[2:]
        where = pl.ds(start, rows)
        for place in range(2 * half):
            read = decoder(coded_ref, place * (share + 1), share)
            peak = jnp.zeros((rows, width), jnp.float32)
            for i in range(share):
                result = kept_ref[place, i] + read(i)
                if place < half:
                    kept[place, i, where] = result
                else:
                    total[i, where] = result
                    peak = jnp.maximum(peak, jnp.abs(result))
            if place >= half:
                encode(lambda i: total[i, where], peak, out, (place - half) * (share + 1), share, where)
        start += rows


def halve(kept, coded, after=()):
    held, share, _, width = kept[0].shape
    rows = sum(k.shape[2] for k in kept)
    return call(
        functools.partial(halve_kernel, len(kept)),
        "halve",
        [VMEM] * (2 * len(kept)),
        [((held // 2, share, rows, width), jnp.float32), ((held // 2 * (share + 1), rows, width), jnp.int16)],
        *kept,
        *coded,
        after=after,
        scratch_shapes=[pltpu.VMEM((share, rows, width), jnp.float32)],
    )


def sum_kernel(counts, *refs):
    *ins, total, out = refs
    share = total.shape[0]
    start = 0
    for count in counts:
        kept, *coded = ins[: 1 + count]
        ins = ins[1 + count :]
        rows = kept.shape[2]
        reads = [decoder(c, 0, share) for c in coded]
        peak = jnp.zeros(kept.shape[2:], jnp.float32)
        where = pl.ds(start, rows)
        for i in range(share):
            result = kept[0, i]
            for read in reads:
                result = result + read(i)
            total[i, where] = result
            peak = jnp.maximum(peak, jnp.abs(result))
        encode(lambda i: total[i, where], peak, out, 0, share, where)
        start += rows


def quarter_sum(groups, after=()):
    _, share, _, width = groups[0][0].shape
    rows = sum(group[0].shape[2] for group in groups)
    args = [array for group in groups for array in group]
    return call(
        functools.partial(sum_kernel, [len(group) - 1 for group in groups]),
        "quarter_sum",
        [VMEM] * len(args),
        [((share, rows, width), jnp.float32), ((share + 1, rows, width), jnp.int16)],
        *args,
        after=after,
    )


def second_kernel(start, own_ref, coded_ref, factor_ref, *rest):
    out_hbm, out, semaphore = rest[-3:]
    share, rows, width = own_ref.shape
    read = decoder(coded_ref, 0, share)
    copies = []
    zero = jnp.zeros((4 * rows, width), jnp.bfloat16)
    for i in range(1, share, 2):
        lines = []
        for j in (i - 1, i):
            values = stacked(own_ref[j], read(j))
            high = values.astype(jnp.bfloat16)
            low = (values - high.astype(jnp.float32)).astype(jnp.bfloat16)
            both = jnp.concatenate([high, low], axis=0)
            lines.append(jnp.concatenate([both, zero] if j < i else [zero, both], axis=1))
        factor = factor_ref[pl.ds(i - 1, 2)].reshape(2 * width, width)
        product = dot(jnp.concatenate(lines, axis=0), factor)
        for j in range(2):
            part = product[4 * rows * j : 4 * rows * (j + 1)]
            out[i - 1 + j] = folded(part[: 2 * rows] + part[2 * rows :])
        if (i + 1) % GROUP == 0:
            some = pl.ds(i + 1 - GROUP, GROUP)
            copy = pltpu.make_async_copy(
                out.at[some], out_hbm.at[some, pl.ds(start, rows)], semaphore.at[i // GROUP]
            )
            copy.start()
            copies.append(copy)
    for copy in copies:
        copy.wait()


def second_level(own, coded, factors, start, rows_in_all, result=None):
    share, rows, width = own.shape
    args = (own, coded, factors) if result is None else (own, coded, factors, result)
    return pl.pallas_call(
        functools.partial(second_kernel, start),
        in_specs=[VMEM] * 3 + [ANY] * (len(args) - 3),
        out_specs=ANY,
        out_shape=jax.ShapeDtypeStruct((share, rows_in_all, width), jnp.float32),
        scratch_shapes=[pltpu.VMEM((share, rows, width), jnp.float32), pltpu.SemaphoreType.DMA((share // GROUP,))],
        input_output_aliases={} if result is None else {3: 0},
        compiler_params=PARAMS,
        name="second_level",
    )(*args)


def on_device(sources, first_factors, second_factors, pattern):
    half = lax.axis_size("tgt") // 2
    parts = lax.axis_size("src")
    sources, first_factors = sources[0], first_factors[0]
    blocks, rows_in_all, _ = sources.shape
    share = blocks // parts
    me = lax.axis_index("src").astype(jnp.int32)
    starts = [sum(CHUNKS[:c]) for c in range(len(CHUNKS))]
    values = [sources[:, : CHUNKS[0]]]
    values += rows_of(sources, CHUNKS[0], CHUNKS[1:], values)
    partners = [swapped(v, "tgt", half) for v in values]
    owns, factors = own_part(values, first_factors)
    mine = lax.dynamic_slice_in_dim(second_factors, me * share, share, 0)
    waiting, marks = {}, {"mine": mine}
    order = [('first', (0,)), ('first', (1,), ('first', (0,))), ('first', (2,), ('first', (1,))), ('halve', (0, 1), ('first', (2,))), ('first', (3,), ('first', (2,)), ('halve', (0, 1))), ('halve', (2,), ('first', (3,)))]
    for step, chunks, *before in order:
        last = [marks[b] for b in before]
        if step == "first":
            (c,) = chunks
            turns = range(1, parts)
            split = [[turn] for turn in turns] if DIRECT[c] else [[turn for turn in turns if turn & 1]]
            kept, *coded = partner_part(split, parts, pattern, owns[c], partners[c], factors, last)
            masks = turns if DIRECT[c] else [1]
            arrived = [swapped(s, "src", mask) for s, mask in zip(coded, masks)]
            waiting[chunks] = (kept, *arrived)
        else:
            kept, coded = halve([waiting[(c,)][0] for c in chunks], [waiting[(c,)][1] for c in chunks], last)
            mask = 2
            arrived = swapped(coded, "src", mask)
            while 2 * mask < parts:
                mask *= 2
                kept, coded = halve([kept], [arrived])
                arrived = swapped(coded, "src", mask)
            waiting[chunks] = (kept, arrived)
        marks[step, chunks] = kept
        marks["arrived", chunks] = waiting[chunks][1]
    result, start = None, 0
    for part in [[(0, 1), (2,)], [(3,)]]:
        total, coded = quarter_sum([waiting[chunks] for chunks in part], ())
        other = swapped(coded, "tgt", half // 2)
        result = second_level(total, other, mine, start, rows_in_all, result)
        start += total.shape[1]
    return result


def solution(mesh):
    return jax.shard_map(
        on_device,
        mesh=mesh,
        in_specs=(
            P("src", "tgt", None, None),
            P("src", "tgt", None, None, None),
            P("tgt", None, None, None),
            P("tgt"),
        ),
        out_specs=P(("tgt", "src"), None, None),
        check_vma=False,
    )
```

```python
import functools

import jax
import jax.numpy as jnp
from jax import lax
from jax.experimental import pallas as pl
from jax.experimental.pallas import tpu as pltpu
from jax.sharding import PartitionSpec as P

CHUNKS = (8, 8, 8, 8)
DIRECT = (0, 0, 0, 1)
GROUP = 8
PACK = 4
VMEM = pl.BlockSpec(memory_space=pltpu.VMEM)
SMEM = pl.BlockSpec(memory_space=pltpu.SMEM)
ANY = pl.BlockSpec(memory_space=pl.ANY)
PARAMS = pltpu.CompilerParams(vmem_limit_bytes=16 << 20)


def swapped(block, axis, mask):
    return lax.ppermute(block, axis, [(i, i ^ mask) for i in range(lax.axis_size(axis))])


def left_half(shape):
    return lax.broadcasted_iota(jnp.int32, shape, len(shape) - 1) < shape[-1] // 2


def turned(values):
    return pltpu.roll(values, values.shape[-1] // 2, 1)


def halves(values):
    values = values.astype(jnp.float32)
    return jnp.concatenate([values, turned(values)], axis=0)[:, : values.shape[-1] // 2].astype(jnp.bfloat16)


def stacked(own, partner):
    left = left_half(own.shape)
    top = jnp.where(left, own, turned(partner))
    bottom = jnp.where(left, turned(own), partner)
    return jnp.concatenate([top, bottom], axis=0)


def folded(product):
    rows = product.shape[0] // 2
    other = turned(product[rows:])
    return product[:rows] + jnp.where(left_half(other.shape), -other, other)


def dot(a, b):
    return jnp.dot(a, b, preferred_element_type=jnp.float32)


def encode(read, peak, out, first, count, where=slice(None)):
    exponent = jnp.floor(jnp.log2(jnp.maximum(peak, 1e-30))) + 1.0
    scale = jnp.exp2(15.0 - exponent)
    for i in range(count):
        code = jnp.clip(jnp.round(read(i) * scale), -32767.0, 32767.0)
        out[first + i, where] = code.astype(jnp.int32).astype(jnp.int16)
    out[first + count, where] = exponent.astype(jnp.int32).astype(jnp.int16)


def decoder(coded, first, count):
    unit = jnp.exp2(coded[first + count].astype(jnp.float32) - 15.0)
    return lambda i: coded[first + i].astype(jnp.float32) * unit


def call(kernel, name, in_specs, outs, *args, after=(), **more):
    count = len(args)

    def body(*refs):
        kernel(*refs[:count], *refs[count + len(after) :])

    return pl.pallas_call(
        body,
        in_specs=in_specs + [ANY] * len(after),
        out_specs=[VMEM] * len(outs),
        out_shape=[jax.ShapeDtypeStruct(shape, kind) for shape, kind in outs],
        compiler_params=PARAMS,
        name=name,
        **more,
    )(*args, *after)


def rows_kernel(start, values_ref, *outs):
    for out in outs:
        rows = out.shape[1]
        out[...] = values_ref[:, pl.ds(start, rows)]
        start += rows


def rows_of(values, start, counts, after=()):
    blocks, _, width = values.shape
    outs = [((blocks, rows, width), values.dtype) for rows in counts]
    return call(functools.partial(rows_kernel, start), "rows_of", [VMEM], outs, values, after=after)


def own_kernel(chunks, *refs):
    values, factor_ref, outs, partner_factors = refs[:chunks], refs[chunks], refs[chunks + 1 : -1], refs[-1]
    for i in range(factor_ref.shape[0]):
        value = jnp.concatenate([v[i].astype(jnp.float32) for v in values], axis=0)
        result = folded(dot(halves(value), factor_ref[i, 0]))
        start = 0
        for out in outs:
            out[i] = result[start : start + out.shape[1]]
            start += out.shape[1]
        partner_factors[i] = factor_ref[i, 1]


def own_part(values, factors):
    blocks, _, rank, width = factors.shape
    outs = [(v.shape, jnp.float32) for v in values] + [((blocks, rank, width), factors.dtype)]
    *owns, partner_factors = call(
        functools.partial(own_kernel, len(values)), "own_part", [VMEM] * (len(values) + 1), outs, *values, factors
    )
    return owns, partner_factors


def partner_kernel(split, pattern_ref, own_ref, partner_ref, factor_ref, kept, *rest):
    *outs, total = rest
    me = lax.axis_index("src")
    share = kept.shape[1]
    rows, width = own_ref.shape[1:]

    left = left_half((rows, width))
    zero = jnp.zeros((2 * rows, width), jnp.bfloat16)

    def blocks(base):
        values = []
        for j in range(PACK):
            value = partner_ref[pattern_ref[base + j]].astype(jnp.float32)
            pair, side = ((value, turned(value)), left) if j % 2 == 0 else ((turned(value), value), ~left)
            column = jnp.concatenate([jnp.where(side, v, 0.0) for v in pair], axis=0).astype(jnp.bfloat16)
            values.append(jnp.concatenate([column if k == j // 2 else zero for k in range(PACK // 2)], axis=1))
        factor = factor_ref[pl.ds(base, PACK)].reshape(PACK * (width // 2), width)
        product = dot(jnp.concatenate(values, axis=0), factor)
        return [own_ref[base + j] + folded(product[2 * rows * j : 2 * rows * (j + 1)]) for j in range(PACK)]

    sent = [turn for turns in split for turn in turns]
    for out, turns in zip(outs, split):
        for place, turn in enumerate(turns):
            peak = jnp.zeros((rows, width), jnp.float32)
            held = total.at[sent.index(turn)]
            for i in range(0, share, PACK):
                for j, result in enumerate(blocks((me ^ turn) * share + i)):
                    held[i + j] = result
                    peak = jnp.maximum(peak, jnp.abs(result))
            encode(lambda i: held[i], peak, out, place * (share + 1), share)
    stay = [turn for turn in range(len(sent) + kept.shape[0]) if turn not in sent]
    for place, turn in enumerate(stay):
        for i in range(0, share, PACK):
            for j, result in enumerate(blocks((me ^ turn) * share + i)):
                kept[place, i + j] = result


def partner_part(split, parts, pattern, own, partner, factors, after=()):
    blocks, rows, width = own.shape
    share = blocks // parts
    sent = sum(len(turns) for turns in split)
    outs = [((parts - sent, share, rows, width), jnp.float32)]
    outs += [((len(turns) * (share + 1), rows, width), jnp.int16) for turns in split]
    return call(
        functools.partial(partner_kernel, split),
        "partner_part",
        [SMEM, VMEM, VMEM, VMEM],
        outs,
        pattern,
        own,
        partner,
        factors,
        after=after,
        scratch_shapes=[pltpu.VMEM((sent, share, rows, width), jnp.float32)],
    )


def halve_kernel(chunks, *refs):
    *ins, kept, out, total = refs
    half, share = kept.shape[:2]
    start = 0
    for kept_ref, coded_ref in zip(ins[:chunks], ins[chunks:]):
        rows, width = kept_ref.shape[2:]
        where = pl.ds(start, rows)
        for place in range(2 * half):
            read = decoder(coded_ref, place * (share + 1), share)
            peak = jnp.zeros((rows, width), jnp.float32)
            for i in range(share):
                result = kept_ref[place, i] + read(i)
                if place < half:
                    kept[place, i, where] = result
                else:
                    total[i, where] = result
                    peak = jnp.maximum(peak, jnp.abs(result))
            if place >= half:
                encode(lambda i: total[i, where], peak, out, (place - half) * (share + 1), share, where)
        start += rows


def halve(kept, coded, after=()):
    held, share, _, width = kept[0].shape
    rows = sum(k.shape[2] for k in kept)
    return call(
        functools.partial(halve_kernel, len(kept)),
        "halve",
        [VMEM] * (2 * len(kept)),
        [((held // 2, share, rows, width), jnp.float32), ((held // 2 * (share + 1), rows, width), jnp.int16)],
        *kept,
        *coded,
        after=after,
        scratch_shapes=[pltpu.VMEM((share, rows, width), jnp.float32)],
    )


def sum_kernel(counts, *refs):
    *ins, total, out = refs
    share = total.shape[0]
    start = 0
    for count in counts:
        kept, *coded = ins[: 1 + count]
        ins = ins[1 + count :]
        rows = kept.shape[2]
        reads = [decoder(c, 0, share) for c in coded]
        peak = jnp.zeros(kept.shape[2:], jnp.float32)
        where = pl.ds(start, rows)
        for i in range(share):
            result = kept[0, i]
            for read in reads:
                result = result + read(i)
            total[i, where] = result
            peak = jnp.maximum(peak, jnp.abs(result))
        encode(lambda i: total[i, where], peak, out, 0, share, where)
        start += rows


def quarter_sum(groups, after=()):
    _, share, _, width = groups[0][0].shape
    rows = sum(group[0].shape[2] for group in groups)
    args = [array for group in groups for array in group]
    return call(
        functools.partial(sum_kernel, [len(group) - 1 for group in groups]),
        "quarter_sum",
        [VMEM] * len(args),
        [((share, rows, width), jnp.float32), ((share + 1, rows, width), jnp.int16)],
        *args,
        after=after,
    )


def second_kernel(start, own_ref, coded_ref, factor_ref, *rest):
    out_hbm, out, semaphore = rest[-3:]
    share, rows, width = own_ref.shape
    read = decoder(coded_ref, 0, share)
    copies = []
    zero = jnp.zeros((4 * rows, width), jnp.bfloat16)
    for i in range(1, share, 2):
        lines = []
        for j in (i - 1, i):
            values = stacked(own_ref[j], read(j))
            high = values.astype(jnp.bfloat16)
            low = (values - high.astype(jnp.float32)).astype(jnp.bfloat16)
            both = jnp.concatenate([high, low], axis=0)
            lines.append(jnp.concatenate([both, zero] if j < i else [zero, both], axis=1))
        factor = factor_ref[pl.ds(i - 1, 2)].reshape(2 * width, width)
        product = dot(jnp.concatenate(lines, axis=0), factor)
        for j in range(2):
            part = product[4 * rows * j : 4 * rows * (j + 1)]
            out[i - 1 + j] = folded(part[: 2 * rows] + part[2 * rows :])
        if (i + 1) % GROUP == 0:
            some = pl.ds(i + 1 - GROUP, GROUP)
            copy = pltpu.make_async_copy(
                out.at[some], out_hbm.at[some, pl.ds(start, rows)], semaphore.at[i // GROUP]
            )
            copy.start()
            copies.append(copy)
    for copy in copies:
        copy.wait()


def second_level(own, coded, factors, start, rows_in_all, result=None):
    share, rows, width = own.shape
    args = (own, coded, factors) if result is None else (own, coded, factors, result)
    return pl.pallas_call(
        functools.partial(second_kernel, start),
        in_specs=[VMEM] * 3 + [ANY] * (len(args) - 3),
        out_specs=ANY,
        out_shape=jax.ShapeDtypeStruct((share, rows_in_all, width), jnp.float32),
        scratch_shapes=[pltpu.VMEM((share, rows, width), jnp.float32), pltpu.SemaphoreType.DMA((share // GROUP,))],
        input_output_aliases={} if result is None else {3: 0},
        compiler_params=PARAMS,
        name="second_level",
    )(*args)


def on_device(sources, first_factors, second_factors, pattern):
    half = lax.axis_size("tgt") // 2
    parts = lax.axis_size("src")
    sources, first_factors = sources[0], first_factors[0]
    blocks, rows_in_all, _ = sources.shape
    share = blocks // parts
    me = lax.axis_index("src").astype(jnp.int32)
    starts = [sum(CHUNKS[:c]) for c in range(len(CHUNKS))]
    values = [sources[:, : CHUNKS[0]]]
    values += rows_of(sources, CHUNKS[0], CHUNKS[1:], values)
    partners = [swapped(v, "tgt", half) for v in values]
    owns, factors = own_part(values, first_factors)
    mine = lax.dynamic_slice_in_dim(second_factors, me * share, share, 0)
    waiting, marks = {}, {"mine": mine}
    order = [('first', (0,)), ('first', (1,), ('first', (0,))), ('first', (2,), ('first', (1,))), ('halve', (0, 1), ('first', (2,))), ('first', (3,), ('first', (2,))), ('halve', (2,), ('first', (3,)))]
    for step, chunks, *before in order:
        last = [marks[b] for b in before]
        if step == "first":
            (c,) = chunks
            turns = range(1, parts)
            split = [[turn] for turn in turns] if DIRECT[c] else [[turn for turn in turns if turn & 1]]
            kept, *coded = partner_part(split, parts, pattern, owns[c], partners[c], factors, last)
            masks = turns if DIRECT[c] else [1]
            arrived = [swapped(s, "src", mask) for s, mask in zip(coded, masks)]
            waiting[chunks] = (kept, *arrived)
        else:
            kept, coded = halve([waiting[(c,)][0] for c in chunks], [waiting[(c,)][1] for c in chunks], last)
            mask = 2
            arrived = swapped(coded, "src", mask)
            while 2 * mask < parts:
                mask *= 2
                kept, coded = halve([kept], [arrived])
                arrived = swapped(coded, "src", mask)
            waiting[chunks] = (kept, arrived)
        marks[step, chunks] = kept
        marks["arrived", chunks] = waiting[chunks][1]
    result, start = None, 0
    for part in [[(0, 1), (2,)], [(3,)]]:
        total, coded = quarter_sum([waiting[chunks] for chunks in part], ())
        other = swapped(coded, "tgt", half // 2)
        result = second_level(total, other, mine, start, rows_in_all, result)
        start += total.shape[1]
    return result


def solution(mesh):
    return jax.shard_map(
        on_device,
        mesh=mesh,
        in_specs=(
            P("src", "tgt", None, None),
            P("src", "tgt", None, None, None),
            P("tgt", None, None, None),
            P("tgt"),
        ),
        out_specs=P(("tgt", "src"), None, None),
        check_vma=False,
    )
```
